128 devices in a mesh: tm: 64 (over z, y, x), space: 2 (over core).
Axes of the slice: x: 4, y: 4, z: 4, core: 2. Of those that a mesh axis runs over, the one named last changes fastest.
Arguments:
- snapshots: bfloat16 [32768, 16384], P('tm', 'space'), may hold values from -40 to 40
- exponents: float32 [2, 32], replicated, may hold values from -150 to 150, as said below
Outputs:
- new_exponents: float32 [2, 32], replicated
- amplitudes: float32 [2, 32, 16384], P(None, None, 'space')
- residual: bfloat16 [32768, 16384], P('tm', 'space')
The draws below stay inside these ranges and needn't reach their ends.
Inputs may be any that keep to these rules, and one draw needn't show every extreme that they name: `exponents`: row 0 lies in -2.3 to 0.8, row 1 in -150 to 150.
All inputs are finite; a program needn't handle non-finite values.
Results may differ from the reference program's by a relative error of at most 0.0012.
The reference program's roundings to bfloat16 on the way count: a program that leaves them out, or rounds other values in their place, can miss the bound.
Values sent between devices are 32-bit elements; how exact they have to be, the bound alone decides.
No kernel may reach another device: no remote copies, remote signals or barrier semaphores. Data moves between devices by JAX's collectives and lax.ppermute only.
A program may use at most 64 MiB of HBM per device.

```python
import math
import jax
import jax.numpy as jnp
from jax import lax

MODES = 32
TIMES = 32768
SPACE = 16384


def true_modes(key):
    base = jax.random.fold_in(key, 7)
    first_key, second_key = jax.random.split(base)
    decay_rates = jax.random.uniform(first_key, (MODES,), jnp.float32, -2.0, 0.5)
    spacing = 2.0 * math.pi * 1.5
    frequencies = spacing * (jnp.arange(MODES, dtype=jnp.float32) - (MODES - 1) / 2.0)
    frequencies = frequencies + jax.random.uniform(second_key, (MODES,), jnp.float32, -2.0, 2.0)
    return (decay_rates, frequencies)


def draw_exponents(key, part):
    decay_rates, frequencies = true_modes(key)
    first_key, second_key = jax.random.split(jax.random.fold_in(key, 19))
    shifted_rates = decay_rates + jax.random.uniform(first_key, (MODES,), jnp.float32, -0.3, 0.3)
    shifted_freqs = frequencies + jax.random.uniform(second_key, (MODES,), jnp.float32, -0.5, 0.5)
    return jnp.stack([shifted_rates, shifted_freqs]).astype(jnp.float32)


def draw_snapshots(key, part):
    decay_rates, frequencies = true_modes(key)
    time_grid = jnp.arange(TIMES, dtype=jnp.int32).astype(jnp.float32) / TIMES
    first_key, second_key = jax.random.split(jax.random.fold_in(key, 23))
    column_pos = jnp.arange(SPACE, dtype=jnp.int32).astype(jnp.float32) / SPACE
    column_scale = 0.15 * (1.0 + 2.0 * column_pos)
    amp_real = jax.random.normal(first_key, (MODES, SPACE), jnp.float32) * column_scale[None, :]
    amp_imag = jax.random.normal(second_key, (MODES, SPACE), jnp.float32) * column_scale[None, :]
    region = jnp.arange(SPACE, dtype=jnp.int32) * 4 // SPACE
    model_part = jnp.zeros((TIMES, SPACE), jnp.float32)
    for quarter in range(4):
        offset = quarter - 1.5
        magnitude = jnp.exp(time_grid[:, None] * (decay_rates + 0.2 * offset)[None, :])
        phase_angle = time_grid[:, None] * (frequencies + 0.8 * offset)[None, :]
        inside = (region == quarter).astype(jnp.float32)[None, :]
        model_part = model_part + jnp.dot(magnitude * jnp.cos(phase_angle), amp_real * inside, precision=lax.Precision.HIGHEST)
        model_part = model_part - jnp.dot(magnitude * jnp.sin(phase_angle), amp_imag * inside, precision=lax.Precision.HIGHEST)
    noise_field = 0.5 * jax.random.normal(jax.random.fold_in(key, 29), (TIMES, SPACE), jnp.float32)
    return jnp.clip(model_part + noise_field, -40.0, 40.0).astype(jnp.bfloat16)


def setup_inputs(seed: int = 0) -> dict:
    key_of = jax.random.split(jax.random.key(seed), 3)
    return {
        "snapshots": draw_snapshots(jax.random.fold_in(key_of[2], 71), 0),
        "exponents": draw_exponents(jax.random.fold_in(key_of[2], 71), 0),
    }


damping = 0.01

def factor_solve(factor, right):
    lower_part = lax.linalg.triangular_solve(factor, right, left_side=True, lower=True)
    return lax.linalg.triangular_solve(factor, lower_part, left_side=True, lower=True, transpose_a=True)

def make_basis(exponents, time_grid):
    magnitude = jnp.exp(time_grid[:, None] * exponents[0][None, :])
    phase_angle = time_grid[:, None] * exponents[1][None, :]
    plain = jnp.concatenate([magnitude * jnp.cos(phase_angle), magnitude * jnp.sin(phase_angle)], 1)
    return jnp.concatenate([plain, time_grid[:, None] * plain], 1)

def inner_product(left, right):
    return lax.dot_general(left.astype(jnp.float32), right.astype(jnp.float32), (((0,), (0,)), ((), ())), precision=lax.Precision.HIGHEST, preferred_element_type=jnp.float32)

def hermitian(blocks, modes):
    return (blocks[:modes, :modes] + blocks[modes:, modes:], blocks[:modes, modes:] - blocks[modes:, :modes])

def embedded(real_part, imag_part):
    return jnp.concatenate([jnp.concatenate([real_part, -imag_part], 1), jnp.concatenate([imag_part, real_part], 1)], 0)

def sign_flip(modes):
    return jnp.concatenate([jnp.ones((modes,), jnp.float32), -jnp.ones((modes,), jnp.float32)])

def basis_solve(gram_matrix, modes):
    double = 2 * modes
    g_real, g_imag = hermitian(gram_matrix[:double, :double], modes)
    factor = jnp.linalg.cholesky(embedded(g_real, g_imag))
    return factor_solve(factor, jnp.eye(double, dtype=jnp.float32))

def amplitude_rows(inverse_g, projections, modes):
    left_solve = inverse_g * sign_flip(modes)[None, :]
    return lax.dot_general(left_solve.astype(jnp.float32), projections[:, :2 * modes].astype(jnp.float32), (((1,), (1,)), ((), ())), precision=lax.Precision.HIGHEST, preferred_element_type=jnp.float32)

def fit_terms(amp_rows, projections, modes):
    double = 2 * modes
    self_terms = lax.dot_general(amp_rows.astype(jnp.float32), amp_rows.astype(jnp.float32), (((1,), (1,)), ((), ())), precision=lax.Precision.HIGHEST, preferred_element_type=jnp.float32)
    cross = jnp.dot(amp_rows.astype(jnp.float32), projections[:, double:].astype(jnp.float32), precision=lax.Precision.HIGHEST, preferred_element_type=jnp.float32) * sign_flip(modes)[None, :]
    v_real = jnp.diagonal(cross[:modes, :modes]) + jnp.diagonal(cross[modes:, modes:])
    v_imag = jnp.diagonal(cross[:modes, modes:]) - jnp.diagonal(cross[modes:, :modes])
    return (self_terms, jnp.stack([v_real, v_imag]))

def lm_update(exponents, gram_matrix, inverse_g, self_terms, cross_sums, modes):
    double = 2 * modes
    c_real, c_imag = hermitian(gram_matrix[:double, double:], modes)
    e_real, e_imag = hermitian(gram_matrix[double:, double:], modes)
    coupling = embedded(c_real, c_imag)
    through = jnp.dot(coupling.T, inverse_g, precision=lax.Precision.HIGHEST)
    reduced = embedded(e_real, e_imag) - jnp.dot(through, coupling, precision=lax.Precision.HIGHEST)
    m_real = reduced[:modes, :modes]
    m_imag = reduced[modes:, :modes]
    s_real, s_imag = hermitian(self_terms, modes)
    w_real = jnp.sum(c_real.T * s_real + c_imag.T * s_imag, 1)
    w_imag = jnp.sum(c_real.T * s_imag - c_imag.T * s_real, 1)
    grad_real = w_real - cross_sums[0]
    grad_imag = w_imag - cross_sums[1]
    h_real = s_real * m_real - s_imag * m_imag + damping * jnp.eye(modes, dtype=jnp.float32)
    h_imag = s_real * m_imag + s_imag * m_real
    factor = jnp.linalg.cholesky(embedded(h_real, h_imag))
    step_vector = factor_solve(factor, jnp.concatenate([grad_real, grad_imag])[:, None])[:, 0]
    return exponents - jnp.stack([step_vector[:modes], step_vector[modes:]])

def reference(snapshots, exponents):
    modes = MODES
    time_grid = jnp.arange(TIMES, dtype=jnp.int32).astype(jnp.float32) / TIMES
    basis = make_basis(exponents, time_grid)
    gram_matrix = inner_product(basis, basis)
    basis_b = basis.astype(jnp.bfloat16)
    projections = lax.dot_general(snapshots.astype(jnp.float32), basis_b.astype(jnp.float32), (((0,), (0,)), ((), ())), preferred_element_type=jnp.float32)
    inverse_g = basis_solve(gram_matrix, modes)
    amp_rows = amplitude_rows(inverse_g, projections, modes)
    self_terms, cross_sums = fit_terms(amp_rows, projections, modes)
    new_exponents = lm_update(exponents, gram_matrix, inverse_g, self_terms, cross_sums, modes)
    signed = (amp_rows * sign_flip(modes)[:, None]).astype(jnp.bfloat16)
    fitted = jnp.dot(basis_b[:, :2 * modes].astype(jnp.float32), signed.astype(jnp.float32), preferred_element_type=jnp.float32)
    residual = (snapshots.astype(jnp.float32) - fitted).astype(jnp.bfloat16)
    return (new_exponents, amp_rows.reshape(2, modes, SPACE), residual)
```

```python
import jax
import jax.numpy as jnp
from jax import lax
from jax.experimental import pallas as pl
from jax.experimental.pallas import tpu as pltpu
from jax.sharding import PartitionSpec as P

damping = 0.01
MODES = 32
TIMES = 32768
ROWS = 512
COLS = 8192
QUARTER = COLS // 4
PART = QUARTER // 4
COARSE = 256
FINE = TIMES // COARSE
EXACT = lax.Precision.HIGHEST
VMEM = pl.BlockSpec(memory_space=pltpu.VMEM)
PARAMS = pltpu.CompilerParams(vmem_limit_bytes=48 * 1024 * 1024)


def place(device):
    return device >> 5, (device >> 3) & 3, (device >> 1) & 3, device & 1


def shifted(axis, step):
    pairs = []
    for device in range(128):
        z, y, x, core = place(device)
        along = "z" if axis == "z" else ("xy" if axis == "u" else "yx")[core]
        if along == "z":
            z = (z + step) % 4
        elif along == "y":
            y = (y + step) % 4
        else:
            x = (x + step) % 4
        pairs.append((device, ((z * 4 + y) * 4 + x) * 2 + core))
    return pairs


def send(value, axis, step):
    return lax.ppermute(value, ("tm", "space"), shifted(axis, step))


def swap_cores(value):
    return lax.ppermute(value, ("tm", "space"), [(d, d ^ 1) for d in range(128)])


def dot(left, right):
    return jnp.dot(left, right, precision=EXACT, preferred_element_type=jnp.float32)


def dot_t(left, right):
    return lax.dot_general(
        left, right, (((1,), (1,)), ((), ())), precision=EXACT, preferred_element_type=jnp.float32
    )


def waves(exponents, times):
    magnitude = jnp.exp(times[None, :] * exponents[0][:, None])
    phase_angle = times[None, :] * exponents[1][:, None]
    return magnitude * jnp.cos(phase_angle), magnitude * jnp.sin(phase_angle)


def table(exponents, times):
    real, imag = waves(exponents, times)
    both = jnp.concatenate([times, times])[None, :]
    plain = jnp.concatenate([real, imag], 1)
    turned = jnp.concatenate([imag, -real], 1)
    return jnp.stack([plain, turned, both * plain, both * turned])


def complex_product(a, b):
    return a[0] * b[0] - a[1] * b[1], a[0] * b[1] + a[1] * b[0]


def eliminate(real, imag, size):
    row_index = lax.broadcasted_iota(jnp.int32, real.shape, 0)
    for k in range(size):
        inverse_pivot = 1.0 / real[k : k + 1, k : k + 1]
        row_real = real[k : k + 1, :] * inverse_pivot
        row_imag = imag[k : k + 1, :] * inverse_pivot
        col_real = real[:, k : k + 1]
        col_imag = imag[:, k : k + 1]
        next_real = real - (col_real * row_real - col_imag * row_imag)
        next_imag = imag - (col_real * row_imag + col_imag * row_real)
        here = row_index == k
        real = jnp.where(here, row_real, next_real)
        imag = jnp.where(here, row_imag, next_imag)
    return real, imag


def grams(t):
    plain, turned, t_plain, t_turned = t[0], t[1], t[2], t[3]
    g = (dot_t(plain, plain), dot_t(plain, turned))
    c = (dot_t(plain, t_plain), dot_t(plain, t_turned))
    ct = (dot_t(t_plain, plain), dot_t(t_turned, plain))
    e = (dot_t(t_plain, t_plain), dot_t(t_plain, t_turned))
    gt = (dot_t(plain, plain), dot_t(turned, plain))
    return g, c, e, gt, ct


def add(a, b):
    return a[0] + b[0], a[1] + b[1]


def gram_kernel(coarse_ref, fine_ref, solve_ref, terms_ref):
    ga, ca, ea, gta, cta = grams(coarse_ref)
    gb, cb, eb, gtb, ctb = grams(fine_ref)
    g = complex_product(ga, gb)
    c = add(complex_product(ca, gb), complex_product(ga, cb))
    ct = add(complex_product(cta, gtb), complex_product(gta, ctb))
    cross = complex_product(ca, cb)
    e = add(complex_product(ea, gb), complex_product(ga, eb))
    e = (e[0] + 2.0 * cross[0], e[1] + 2.0 * cross[1])
    row = lax.broadcasted_iota(jnp.int32, (MODES, MODES), 0)
    col = lax.broadcasted_iota(jnp.int32, (MODES, MODES), 1)
    one = (row == col).astype(jnp.float32)
    real = jnp.concatenate([g[0], one], 1)
    imag = jnp.concatenate([g[1], jnp.zeros_like(one)], 1)
    real, imag = eliminate(real, imag, MODES)
    inv_real, inv_imag = real[:, MODES:], imag[:, MODES:]
    solve_ref[...] = jnp.concatenate(
        [jnp.concatenate([inv_real, inv_imag], 1), jnp.concatenate([inv_imag, -inv_real], 1)], 0
    )
    d_real = dot(inv_real, c[0]) - dot(inv_imag, c[1])
    d_imag = dot(inv_real, c[1]) + dot(inv_imag, c[0])
    terms_ref[0] = e[0] - (dot(ct[0], d_real) + dot(ct[1], d_imag))
    terms_ref[1] = e[1] - (dot(ct[0], d_imag) - dot(ct[1], d_real))
    terms_ref[2] = ct[0]
    terms_ref[3] = ct[1]


def project_kernel(index_ref, basis_ref, snapshots_ref, out_ref):
    out_ref[0] = jnp.dot(
        basis_ref[...], snapshots_ref[...], preferred_element_type=jnp.float32
    )


def project(index, basis_t, snapshots):
    return pl.pallas_call(
        project_kernel,
        grid_spec=pltpu.PrefetchScalarGridSpec(
            num_scalar_prefetch=1,
            grid=(4,),
            in_specs=[
                pl.BlockSpec((4 * MODES, ROWS), lambda j, i: (0, 0)),
                pl.BlockSpec((ROWS, PART), lambda j, i: (0, i[0] * 4 + j)),
            ],
            out_specs=pl.BlockSpec((1, 4 * MODES, PART), lambda j, i: (j, 0, 0)),
        ),
        out_shape=jax.ShapeDtypeStruct((4, 4 * MODES, PART), jnp.float32),
        compiler_params=PARAMS,
        cost_estimate=pl.CostEstimate(
            flops=2 * 128 * ROWS * QUARTER, bytes_accessed=3 << 20, transcendentals=0
        ),
        name="project",
    )(index, basis_t, snapshots)


def first_sum_kernel(v_ref, own_ref, r1_ref, r2_ref, r3_ref, *out_refs):
    for step in range(4):
        j = (v_ref[0] + step) & 3
        out_refs[step][...] = (own_ref[j] + r2_ref[j]) + (r1_ref[j] + r3_ref[j])


def first_sum(v, own, received):
    return pl.pallas_call(
        first_sum_kernel,
        in_specs=[pl.BlockSpec(memory_space=pltpu.SMEM)] + [VMEM] * 4,
        out_specs=[VMEM] * 4,
        out_shape=[jax.ShapeDtypeStruct((4 * MODES, PART), jnp.float32)] * 4,
        compiler_params=PARAMS,
        name="first_sum",
    )(v, own, *received)


def sum_kernel(own_ref, r1_ref, r2_ref, r3_ref, out_ref):
    out_ref[...] = (own_ref[...] + r2_ref[...]) + (r1_ref[...] + r3_ref[...])


def plain_sum(own, received):
    return pl.pallas_call(
        sum_kernel,
        in_specs=[VMEM] * 4,
        out_specs=VMEM,
        out_shape=jax.ShapeDtypeStruct(own.shape, jnp.float32),
        compiler_params=PARAMS,
        name="plain_sum",
    )(own, *received)


def amplitude_kernel(solve_ref, own_ref, r1_ref, r2_ref, r3_ref, out_ref):
    total = (own_ref[...] + r2_ref[...]) + (r1_ref[...] + r3_ref[...])
    amp = dot(solve_ref[...], total[: 2 * MODES])
    out_ref[:, :PART] = amp
    amp_real, amp_imag = amp[:MODES], amp[MODES:]
    z_cos, z_sin = total[2 * MODES : 3 * MODES], total[3 * MODES :]
    v_real = jnp.sum(amp_real * z_cos - amp_imag * z_sin, 1, keepdims=True)
    v_imag = jnp.sum(-amp_real * z_sin - amp_imag * z_cos, 1, keepdims=True)
    v = jnp.concatenate([v_real, v_imag], 0)
    s = dot_t(amp, amp)
    out_ref[:, PART:] = jnp.concatenate([s, jnp.broadcast_to(v, (64, 64))], 1)


def amplitudes_of(solve, own, received):
    return pl.pallas_call(
        amplitude_kernel,
        in_specs=[VMEM] * 5,
        out_specs=VMEM,
        out_shape=jax.ShapeDtypeStruct((2 * MODES, PART + 128), jnp.float32),
        compiler_params=PARAMS,
        name="amplitudes",
    )(solve, own, *received)


def join_kernel(v_ref, own_ref, r1_ref, r2_ref, r3_ref, out_ref):
    for step, ref in enumerate((own_ref, r1_ref, r2_ref, r3_ref)):
        j = (v_ref[0] - step) & 3
        out_ref[:, pl.ds(pl.multiple_of(j * PART, PART), PART)] = ref[:, :PART]
    out_ref[:, QUARTER:] = (own_ref[:, PART:] + r2_ref[:, PART:]) + (
        r1_ref[:, PART:] + r3_ref[:, PART:]
    )


def join(v, own, received):
    return pl.pallas_call(
        join_kernel,
        in_specs=[pl.BlockSpec(memory_space=pltpu.SMEM)] + [VMEM] * 4,
        out_specs=VMEM,
        out_shape=jax.ShapeDtypeStruct((2 * MODES, QUARTER + 128), jnp.float32),
        compiler_params=PARAMS,
        name="join",
    )(v, own, *received)


def residual_kernel(index_ref, basis_ref, amp_ref, snapshots_ref, *refs):
    residual_ref, amp_out_ref = refs[-2:]
    amp = amp_ref[...]
    amp_out_ref[...] = amp
    signed = jnp.concatenate([amp[:MODES], -amp[MODES:]], 0).astype(jnp.bfloat16)
    fitted = jnp.dot(basis_ref[...], signed, preferred_element_type=jnp.float32)
    residual_ref[...] = (snapshots_ref[...].astype(jnp.float32) - fitted).astype(jnp.bfloat16)


def residual_part(index, basis, amp, snapshots, before):
    kept = [] if before is None else list(before)
    return pl.pallas_call(
        residual_kernel,
        grid_spec=pltpu.PrefetchScalarGridSpec(
            num_scalar_prefetch=1,
            grid=(4,),
            in_specs=[
                pl.BlockSpec((ROWS, 2 * MODES), lambda j, i: (0, 0)),
                pl.BlockSpec((2 * MODES, PART), lambda j, i: (0, j)),
                pl.BlockSpec((ROWS, PART), lambda j, i: (0, i[0] * 4 + j)),
            ]
            + [pl.BlockSpec(memory_space=pl.ANY)] * len(kept),
            out_specs=[
                pl.BlockSpec((ROWS, PART), lambda j, i: (0, i[0] * 4 + j)),
                pl.BlockSpec((2 * MODES, PART), lambda j, i: (0, i[0] * 4 + j)),
            ],
        ),
        out_shape=[
            jax.ShapeDtypeStruct((ROWS, COLS), jnp.bfloat16),
            jax.ShapeDtypeStruct((2 * MODES, COLS), jnp.float32),
        ],
        input_output_aliases={4: 0, 5: 1} if kept else {},
        compiler_params=PARAMS,
        cost_estimate=pl.CostEstimate(
            flops=2 * 64 * ROWS * QUARTER, bytes_accessed=5 << 20, transcendentals=0
        ),
        name="residual_part",
    )(index, basis, amp, snapshots, *kept)


def update_kernel(exponents_ref, terms_ref, here_ref, there_ref, out_ref):
    total = here_ref[...] + there_ref[...]
    s_real = total[:MODES, :MODES] + total[MODES:, MODES : 2 * MODES]
    s_imag = total[:MODES, MODES : 2 * MODES] - total[MODES:, :MODES]
    v_real = total[:MODES, 2 * MODES : 2 * MODES + 1]
    v_imag = total[MODES:, 2 * MODES : 2 * MODES + 1]
    m_real, m_imag, ct_real, ct_imag = (terms_ref[i] for i in range(4))
    row = lax.broadcasted_iota(jnp.int32, (MODES, MODES), 0)
    col = lax.broadcasted_iota(jnp.int32, (MODES, MODES), 1)
    one = (row == col).astype(jnp.float32)
    w_real = jnp.sum(ct_real * s_real + ct_imag * s_imag, 1, keepdims=True)
    w_imag = jnp.sum(ct_real * s_imag - ct_imag * s_real, 1, keepdims=True)
    h_real = s_real * m_real - s_imag * m_imag + damping * one
    h_imag = s_real * m_imag + s_imag * m_real
    wide = (MODES, MODES)
    real = jnp.concatenate([h_real, jnp.broadcast_to(w_real - v_real, wide)], 1)
    imag = jnp.concatenate([h_imag, jnp.broadcast_to(w_imag - v_imag, wide)], 1)
    real, imag = eliminate(real, imag, MODES)
    step_real = jnp.sum(one * real[:, MODES:], 0, keepdims=True)
    step_imag = jnp.sum(one * imag[:, MODES:], 0, keepdims=True)
    out_ref[...] = exponents_ref[...] - jnp.concatenate([step_real, step_imag], 0)


def shards(snapshots, exponents):
    z, y, x, core = place(lax.axis_index("tm") * 2 + lax.axis_index("space"))
    u = jnp.where(core == 0, x, y).astype(jnp.int32)
    v = jnp.where(core == 0, y, x).astype(jnp.int32)
    at_v = v[None]
    first_row = lax.axis_index("tm") * ROWS
    times = (first_row + jnp.arange(ROWS, dtype=jnp.int32)).astype(jnp.float32) / TIMES
    real, imag = waves(exponents, times)
    basis_t = jnp.concatenate([real, imag], 0)
    basis_t = jnp.concatenate([basis_t, times[None, :] * basis_t], 0).astype(jnp.bfloat16)
    basis = basis_t[: 2 * MODES].T

    received = {}
    for step in (2, 1, 3):
        part = project(((u + step) & 3)[None], basis_t, snapshots)
        received[step] = send(part, "u", step)
    own = project(u[None], basis_t, snapshots)

    coarse = table(exponents, jnp.arange(COARSE, dtype=jnp.float32) / COARSE)
    fine = table(exponents, jnp.arange(FINE, dtype=jnp.float32) / TIMES)
    solve, terms = pl.pallas_call(
        gram_kernel,
        in_specs=[VMEM] * 2,
        out_specs=[VMEM] * 2,
        out_shape=[
            jax.ShapeDtypeStruct((2 * MODES, 2 * MODES), jnp.float32),
            jax.ShapeDtypeStruct((4, MODES, MODES), jnp.float32),
        ],
        compiler_params=PARAMS,
        cost_estimate=pl.CostEstimate(
            flops=1 << 30, bytes_accessed=16 << 20, transcendentals=0
        ),
        name="gram",
    )(coarse, fine)

    sums = first_sum(at_v, own, [received[s] for s in (1, 2, 3)])
    received = {s: send(sums[s], "v", s) for s in (2, 1, 3)}
    total = plain_sum(sums[0], [received[s] for s in (1, 2, 3)])
    received = {s: send(total, "z", s) for s in (2, 1, 3)}
    amp = amplitudes_of(solve, total, [received[s] for s in (1, 2, 3)])
    received = {s: send(amp, "v", s) for s in (2, 1, 3)}
    amp = join(at_v, amp, [received[s] for s in (1, 2, 3)])
    received = {s: send(amp, "u", s) for s in (2, 1, 3)}
    out = residual_part(u[None], basis, amp, snapshots, None)
    sums = plain_sum(
        amp[:, QUARTER:], [received[s][:, QUARTER:] for s in (1, 2, 3)]
    )
    other = swap_cores(sums)
    for step in (1, 3, 2):
        out = residual_part(((u - step) & 3)[None], basis, received[step], snapshots, out)
    residual, amp = out
    new_exponents = pl.pallas_call(
        update_kernel,
        in_specs=[VMEM] * 4,
        out_specs=VMEM,
        out_shape=jax.ShapeDtypeStruct((2, MODES), jnp.float32),
        compiler_params=PARAMS,
        name="update",
    )(exponents, terms, sums, other)
    return (new_exponents, amp.reshape(2, MODES, COLS), residual)


def solution(mesh):
    return jax.shard_map(
        shards,
        mesh=mesh,
        in_specs=(P("tm", "space"), P()),
        out_specs=(P(), P(None, None, "space"), P("tm", "space")),
        check_vma=False,
    )
```

```python
import jax
import jax.numpy as jnp
from jax import lax
from jax.experimental import pallas as pl
from jax.experimental.pallas import tpu as pltpu
from jax.sharding import PartitionSpec as P

damping = 0.01
MODES = 32
TIMES = 32768
ROWS = 512
COLS = 8192
QUARTER = COLS // 4
PART = QUARTER // 4
WIDTH = 512
ORDER = (1, 3, 2)
COARSE = 256
FINE = TIMES // COARSE
EXACT = lax.Precision.HIGHEST
VMEM = pl.BlockSpec(memory_space=pltpu.VMEM)
PARAMS = pltpu.CompilerParams(vmem_limit_bytes=24 * 1024 * 1024)
WIDE_PARAMS = pltpu.CompilerParams(vmem_limit_bytes=52 * 1024 * 1024)
AXES = {"u": "xy", "v": "yz", "w": "zx"}


def place(device):
    return device >> 5, (device >> 3) & 3, (device >> 1) & 3, device & 1


def shifted(axis, step):
    pairs = []
    for device in range(128):
        z, y, x, core = place(device)
        along = AXES[axis][core]
        if along == "z":
            z = (z + step) % 4
        elif along == "y":
            y = (y + step) % 4
        else:
            x = (x + step) % 4
        pairs.append((device, ((z * 4 + y) * 4 + x) * 2 + core))
    return pairs


def send(value, axis, step):
    return lax.ppermute(value, ("tm", "space"), shifted(axis, step))


def swap_cores(value):
    return lax.ppermute(value, ("tm", "space"), [(d, d ^ 1) for d in range(128)])


def dot(left, right):
    return jnp.dot(left, right, precision=EXACT, preferred_element_type=jnp.float32)


def dot_t(left, right):
    return lax.dot_general(
        left, right, (((1,), (1,)), ((), ())), precision=EXACT, preferred_element_type=jnp.float32
    )


def waves(exponents, times):
    magnitude = jnp.exp(times[None, :] * exponents[0][:, None])
    phase_angle = times[None, :] * exponents[1][:, None]
    return magnitude * jnp.cos(phase_angle), magnitude * jnp.sin(phase_angle)


def basis_kernel(first_ref, exponents_ref, flat_ref, tall_ref):
    row = lax.broadcasted_iota(jnp.int32, (MODES, MODES), 0)
    col = lax.broadcasted_iota(jnp.int32, (MODES, MODES), 1)
    values = exponents_ref[...]
    rate = jnp.sum(jnp.where(row == col, values[0:1], 0.0), 1, keepdims=True)
    frequency = jnp.sum(jnp.where(row == col, values[1:2], 0.0), 1, keepdims=True)
    step = first_ref[0] + lax.broadcasted_iota(jnp.int32, (MODES, ROWS), 1)
    times = step.astype(jnp.float32) * (1.0 / TIMES)
    magnitude = jnp.exp(times * rate)
    phase_angle = times * frequency
    real = magnitude * jnp.cos(phase_angle)
    imag = magnitude * jnp.sin(phase_angle)
    plain = jnp.concatenate([real, imag], 0)
    flat_ref[...] = jnp.concatenate([plain, times * real, times * imag], 0).astype(jnp.bfloat16)
    tall_ref[...] = plain.T.astype(jnp.bfloat16)


def make_basis(first_row, exponents):
    return pl.pallas_call(
        basis_kernel,
        in_specs=[pl.BlockSpec(memory_space=pltpu.SMEM), VMEM],
        out_specs=[VMEM] * 2,
        out_shape=[
            jax.ShapeDtypeStruct((4 * MODES, ROWS), jnp.bfloat16),
            jax.ShapeDtypeStruct((ROWS, 2 * MODES), jnp.bfloat16),
        ],
        compiler_params=PARAMS,
        name="basis",
    )(first_row.astype(jnp.int32), exponents)


def table(exponents, times):
    real, imag = waves(exponents, times)
    both = jnp.concatenate([times, times])[None, :]
    plain = jnp.concatenate([real, imag], 1)
    turned = jnp.concatenate([imag, -real], 1)
    return jnp.stack([plain, turned, both * plain, both * turned])


def complex_product(a, b):
    return a[0] * b[0] - a[1] * b[1], a[0] * b[1] + a[1] * b[0]


def eliminate(real, imag, size):
    row_index = lax.broadcasted_iota(jnp.int32, real.shape, 0)
    for k in range(size):
        inverse_pivot = 1.0 / real[k : k + 1, k : k + 1]
        row_real = real[k : k + 1, :] * inverse_pivot
        row_imag = imag[k : k + 1, :] * inverse_pivot
        col_real = real[:, k : k + 1]
        col_imag = imag[:, k : k + 1]
        next_real = real - (col_real * row_real - col_imag * row_imag)
        next_imag = imag - (col_real * row_imag + col_imag * row_real)
        here = row_index == k
        real = jnp.where(here, row_real, next_real)
        imag = jnp.where(here, row_imag, next_imag)
    return real, imag


def grams(t):
    plain, turned, t_plain, t_turned = t[0], t[1], t[2], t[3]
    g = (dot_t(plain, plain), dot_t(plain, turned))
    c = (dot_t(plain, t_plain), dot_t(plain, t_turned))
    ct = (dot_t(t_plain, plain), dot_t(t_turned, plain))
    e = (dot_t(t_plain, t_plain), dot_t(t_plain, t_turned))
    gt = (dot_t(plain, plain), dot_t(turned, plain))
    return g, c, e, gt, ct


def add(a, b):
    return a[0] + b[0], a[1] + b[1]


def gram_kernel(coarse_ref, fine_ref, solve_ref, terms_ref):
    ga, ca, ea, gta, cta = grams(coarse_ref)
    gb, cb, eb, gtb, ctb = grams(fine_ref)
    g = complex_product(ga, gb)
    c = add(complex_product(ca, gb), complex_product(ga, cb))
    ct = add(complex_product(cta, gtb), complex_product(gta, ctb))
    cross = complex_product(ca, cb)
    e = add(complex_product(ea, gb), complex_product(ga, eb))
    e = (e[0] + 2.0 * cross[0], e[1] + 2.0 * cross[1])
    row = lax.broadcasted_iota(jnp.int32, (MODES, MODES), 0)
    col = lax.broadcasted_iota(jnp.int32, (MODES, MODES), 1)
    one = (row == col).astype(jnp.float32)
    real = jnp.concatenate([g[0], one], 1)
    imag = jnp.concatenate([g[1], jnp.zeros_like(one)], 1)
    real, imag = eliminate(real, imag, MODES)
    inv_real, inv_imag = real[:, MODES:], imag[:, MODES:]
    solve_ref[...] = jnp.concatenate(
        [jnp.concatenate([inv_real, inv_imag], 1), jnp.concatenate([inv_imag, -inv_real], 1)], 0
    )
    d_real = dot(inv_real, c[0]) - dot(inv_imag, c[1])
    d_imag = dot(inv_real, c[1]) + dot(inv_imag, c[0])
    terms_ref[0] = e[0] - (dot(ct[0], d_real) + dot(ct[1], d_imag))
    terms_ref[1] = e[1] - (dot(ct[0], d_imag) - dot(ct[1], d_real))
    terms_ref[2] = ct[0]
    terms_ref[3] = ct[1]


def project_kernel(index_ref, basis_ref, snapshots_ref, *out_refs):
    for step, out_ref in enumerate(out_refs):

        @pl.when(pl.program_id(0) == step)
        def _():
            found = jnp.dot(
                basis_ref[...], snapshots_ref[...], preferred_element_type=jnp.float32
            )
            for j in range(4):
                out_ref[j] = found[:, j * PART : (j + 1) * PART]


def project(indices, basis_t, snapshots):
    count = indices.shape[0]
    return pl.pallas_call(
        project_kernel,
        grid_spec=pltpu.PrefetchScalarGridSpec(
            num_scalar_prefetch=1,
            grid=(count,),
            in_specs=[
                pl.BlockSpec((4 * MODES, ROWS), lambda j, i: (0, 0)),
                pl.BlockSpec((ROWS, QUARTER), lambda j, i: (0, i[j])),
            ],
            out_specs=[pl.BlockSpec((4, 4 * MODES, PART), lambda j, i: (0, 0, 0))] * count,
        ),
        out_shape=[jax.ShapeDtypeStruct((4, 4 * MODES, PART), jnp.float32)] * count,
        compiler_params=WIDE_PARAMS,
        cost_estimate=pl.CostEstimate(
            flops=count * 2 * 128 * ROWS * QUARTER,
            bytes_accessed=count * (3 << 20),
            transcendentals=0,
        ),
        name="project",
    )(indices, basis_t, snapshots)


def first_sum_kernel(v_ref, own_ref, r1_ref, r2_ref, r3_ref, *out_refs):
    for step in range(4):
        j = (v_ref[0] + step) & 3
        out_refs[step][...] = (own_ref[j] + r2_ref[j]) + (r1_ref[j] + r3_ref[j])


def first_sum(v, own, received):
    return pl.pallas_call(
        first_sum_kernel,
        in_specs=[pl.BlockSpec(memory_space=pltpu.SMEM)] + [VMEM] * 4,
        out_specs=[VMEM] * 4,
        out_shape=[jax.ShapeDtypeStruct((4 * MODES, PART), jnp.float32)] * 4,
        compiler_params=PARAMS,
        name="first_sum",
    )(v, own, *received)


def sum_kernel(own_ref, r1_ref, r2_ref, r3_ref, out_ref):
    out_ref[...] = (own_ref[...] + r2_ref[...]) + (r1_ref[...] + r3_ref[...])


def plain_sum(own, received):
    return pl.pallas_call(
        sum_kernel,
        in_specs=[VMEM] * 4,
        out_specs=VMEM,
        out_shape=jax.ShapeDtypeStruct(own.shape, jnp.float32),
        compiler_params=PARAMS,
        name="plain_sum",
    )(own, *received)


def amplitude_kernel(solve_ref, own_ref, r1_ref, r2_ref, r3_ref, out_ref):
    total = (own_ref[...] + r2_ref[...]) + (r1_ref[...] + r3_ref[...])
    amp = dot(solve_ref[...], total[: 2 * MODES])
    out_ref[:, :PART] = amp
    amp_real, amp_imag = amp[:MODES], amp[MODES:]
    z_cos, z_sin = total[2 * MODES : 3 * MODES], total[3 * MODES :]
    v_real = jnp.sum(amp_real * z_cos - amp_imag * z_sin, 1, keepdims=True)
    v_imag = jnp.sum(-amp_real * z_sin - amp_imag * z_cos, 1, keepdims=True)
    v = jnp.concatenate([v_real, v_imag], 0)
    s = dot_t(amp, amp)
    out_ref[:, PART:] = jnp.concatenate([s, jnp.broadcast_to(v, (64, 64))], 1)


def amplitudes_of(solve, own, received):
    return pl.pallas_call(
        amplitude_kernel,
        in_specs=[VMEM] * 5,
        out_specs=VMEM,
        out_shape=jax.ShapeDtypeStruct((2 * MODES, PART + 128), jnp.float32),
        compiler_params=PARAMS,
        name="amplitudes",
    )(solve, own, *received)


def join_kernel(v_ref, own_ref, r1_ref, r2_ref, r3_ref, out_ref):
    for step, ref in enumerate((own_ref, r1_ref, r2_ref, r3_ref)):
        j = (v_ref[0] - step) & 3
        out_ref[:, pl.ds(pl.multiple_of(j * PART, PART), PART)] = ref[:, :PART]
    out_ref[:, QUARTER:] = (own_ref[:, PART:] + r2_ref[:, PART:]) + (
        r1_ref[:, PART:] + r3_ref[:, PART:]
    )


def join(v, own, received):
    return pl.pallas_call(
        join_kernel,
        in_specs=[pl.BlockSpec(memory_space=pltpu.SMEM)] + [VMEM] * 4,
        out_specs=VMEM,
        out_shape=jax.ShapeDtypeStruct((2 * MODES, QUARTER + 128), jnp.float32),
        compiler_params=PARAMS,
        name="join",
    )(v, own, *received)


def columns_of(quarter):
    return pl.ds(pl.multiple_of(quarter * QUARTER, QUARTER), QUARTER)


def fit_piece(basis_ref, amp_ref, snapshots_ref, out_ref):
    for first in range(0, QUARTER, WIDTH):
        here = pl.ds(first, WIDTH)
        amp = amp_ref[:, here]
        signed = jnp.concatenate([amp[:MODES], -amp[MODES:]], 0).astype(jnp.bfloat16)
        fitted = jnp.dot(basis_ref[...], signed, preferred_element_type=jnp.float32)
        out_ref[:, here] = (snapshots_ref[:, here].astype(jnp.float32) - fitted).astype(
            jnp.bfloat16
        )


def own_kernel(
    u_ref, basis_ref, amp_ref, snapshots_ref, residual_ref, amp_out_ref, rest_ref, old, new, sems
):
    own = columns_of(u_ref[0])
    load = pltpu.make_async_copy(snapshots_ref.at[:, own], old, sems.at[0])
    load.start()
    copies = [
        pltpu.make_async_copy(amp_ref.at[:, pl.ds(0, QUARTER)], amp_out_ref.at[:, own], sems.at[1])
    ]
    for n, step in enumerate(ORDER):
        there = columns_of((u_ref[0] - step) & 3)
        copies.append(
            pltpu.make_async_copy(snapshots_ref.at[:, there], rest_ref.at[n], sems.at[2 + n])
        )
    for copy in copies:
        copy.start()
    load.wait()
    fit_piece(basis_ref, amp_ref, old, new)
    store = pltpu.make_async_copy(new, residual_ref.at[:, own], sems.at[0])
    store.start()
    for copy in copies:
        copy.wait()
    store.wait()


def rest_kernel(u_ref, basis_ref, a1, a2, a3, rest_ref, k1, k2, residual_ref, amp_out_ref, new, sems):
    copies = []
    for n, (step, amp_ref) in enumerate(zip(ORDER, (a1, a2, a3))):
        there = columns_of((u_ref[0] - step) & 3)
        copies.append(
            pltpu.make_async_copy(
                amp_ref.at[:, pl.ds(0, QUARTER)], amp_out_ref.at[:, there], sems.at[n]
            )
        )
        copies[-1].start()
    for n, (step, amp_ref) in enumerate(zip(ORDER, (a1, a2, a3))):
        there = columns_of((u_ref[0] - step) & 3)
        fit_piece(basis_ref, amp_ref, rest_ref.at[n], new.at[n])
        copies.append(
            pltpu.make_async_copy(new.at[n], residual_ref.at[:, there], sems.at[3 + n])
        )
        copies[-1].start()
    for copy in copies:
        copy.wait()


SMEM = pl.BlockSpec(memory_space=pltpu.SMEM)
HBM = pl.BlockSpec(memory_space=pltpu.HBM)
RESULTS = [
    jax.ShapeDtypeStruct((ROWS, COLS), jnp.bfloat16),
    jax.ShapeDtypeStruct((2 * MODES, COLS), jnp.float32),
]


def own_residual(u, basis, amp, snapshots):
    return pl.pallas_call(
        own_kernel,
        in_specs=[SMEM, VMEM, VMEM, HBM],
        out_specs=[HBM, HBM, VMEM],
        out_shape=RESULTS + [jax.ShapeDtypeStruct((3, ROWS, QUARTER), jnp.bfloat16)],
        scratch_shapes=[
            pltpu.VMEM((ROWS, QUARTER), jnp.bfloat16),
            pltpu.VMEM((ROWS, QUARTER), jnp.bfloat16),
            pltpu.SemaphoreType.DMA((5,)),
        ],
        compiler_params=PARAMS,
        cost_estimate=pl.CostEstimate(
            flops=2 * 64 * ROWS * QUARTER, bytes_accessed=11 << 20, transcendentals=0
        ),
        name="own_residual",
    )(u, basis, amp, snapshots)


def rest_residual(u, basis, amps, rest, residual, amp_out):
    return pl.pallas_call(
        rest_kernel,
        in_specs=[SMEM, VMEM, VMEM, VMEM, VMEM, VMEM, HBM, HBM],
        out_specs=[HBM, HBM],
        out_shape=RESULTS,
        input_output_aliases={6: 0, 7: 1},
        scratch_shapes=[
            pltpu.VMEM((3, ROWS, QUARTER), jnp.bfloat16),
            pltpu.SemaphoreType.DMA((6,)),
        ],
        compiler_params=PARAMS,
        cost_estimate=pl.CostEstimate(
            flops=6 * 64 * ROWS * QUARTER, bytes_accessed=8 << 20, transcendentals=0
        ),
        name="rest_residual",
    )(u, basis, *amps, rest, residual, amp_out)


def update_kernel(exponents_ref, terms_ref, here_ref, there_ref, out_ref):
    total = here_ref[...] + there_ref[...]
    s_real = total[:MODES, :MODES] + total[MODES:, MODES : 2 * MODES]
    s_imag = total[:MODES, MODES : 2 * MODES] - total[MODES:, :MODES]
    v_real = total[:MODES, 2 * MODES : 2 * MODES + 1]
    v_imag = total[MODES:, 2 * MODES : 2 * MODES + 1]
    m_real, m_imag, ct_real, ct_imag = (terms_ref[i] for i in range(4))
    row = lax.broadcasted_iota(jnp.int32, (MODES, MODES), 0)
    col = lax.broadcasted_iota(jnp.int32, (MODES, MODES), 1)
    one = (row == col).astype(jnp.float32)
    w_real = jnp.sum(ct_real * s_real + ct_imag * s_imag, 1, keepdims=True)
    w_imag = jnp.sum(ct_real * s_imag - ct_imag * s_real, 1, keepdims=True)
    h_real = s_real * m_real - s_imag * m_imag + damping * one
    h_imag = s_real * m_imag + s_imag * m_real
    wide = (MODES, MODES)
    real = jnp.concatenate([h_real, jnp.broadcast_to(w_real - v_real, wide)], 1)
    imag = jnp.concatenate([h_imag, jnp.broadcast_to(w_imag - v_imag, wide)], 1)
    real, imag = eliminate(real, imag, MODES)
    step_real = jnp.sum(one * real[:, MODES:], 0, keepdims=True)
    step_imag = jnp.sum(one * imag[:, MODES:], 0, keepdims=True)
    out_ref[...] = exponents_ref[...] - jnp.concatenate([step_real, step_imag], 0)


def shards(snapshots, exponents):
    z, y, x, core = place(lax.axis_index("tm") * 2 + lax.axis_index("space"))
    u = jnp.where(core == 0, x, y).astype(jnp.int32)
    v = jnp.where(core == 0, y, z).astype(jnp.int32)
    at_v = v[None]
    basis_t, basis = make_basis(lax.axis_index("tm")[None] * ROWS, exponents)

    received = {}
    (part,) = project(((u + 2) & 3)[None], basis_t, snapshots)
    received[2] = send(part, "u", 2)
    others = project(jnp.stack([(u + 1) & 3, (u + 3) & 3]), basis_t, snapshots)
    received[1] = send(others[0], "u", 1)
    received[3] = send(others[1], "u", 3)
    (own,) = project(u[None], basis_t, snapshots)

    coarse = table(exponents, jnp.arange(COARSE, dtype=jnp.float32) / COARSE)
    fine = table(exponents, jnp.arange(FINE, dtype=jnp.float32) / TIMES)
    solve, terms = pl.pallas_call(
        gram_kernel,
        in_specs=[VMEM] * 2,
        out_specs=[VMEM] * 2,
        out_shape=[
            jax.ShapeDtypeStruct((2 * MODES, 2 * MODES), jnp.float32),
            jax.ShapeDtypeStruct((4, MODES, MODES), jnp.float32),
        ],
        compiler_params=PARAMS,
        cost_estimate=pl.CostEstimate(
            flops=1 << 30, bytes_accessed=16 << 20, transcendentals=0
        ),
        name="gram",
    )(coarse, fine)

    own, solve, terms = lax.optimization_barrier((own, solve, terms))
    sums = first_sum(at_v, own, [received[s] for s in (1, 2, 3)])
    received = {s: send(sums[s], "v", s) for s in (2, 1, 3)}
    total = plain_sum(sums[0], [received[s] for s in (1, 2, 3)])
    received = {s: send(total, "w", s) for s in (2, 1, 3)}
    amp = amplitudes_of(solve, total, [received[s] for s in (1, 2, 3)])
    received = {s: send(amp, "v", s) for s in (2, 1, 3)}
    amp = join(at_v, amp, [received[s] for s in (1, 2, 3)])
    received = {s: send(amp, "u", s) for s in (2, 1, 3)}
    residual, amp_out, rest = own_residual(u[None], basis, amp, snapshots)
    sums = plain_sum(
        amp[:, QUARTER:], [received[s][:, QUARTER:] for s in (1, 2, 3)]
    )
    other = swap_cores(sums)
    residual, amp_out = rest_residual(
        u[None], basis, [received[step] for step in ORDER], rest, residual, amp_out
    )
    new_exponents = pl.pallas_call(
        update_kernel,
        in_specs=[VMEM] * 4,
        out_specs=VMEM,
        out_shape=jax.ShapeDtypeStruct((2, MODES), jnp.float32),
        compiler_params=PARAMS,
        name="update",
    )(exponents, terms, sums, other)
    return (new_exponents, amp_out.reshape(2, MODES, COLS), residual)


def solution(mesh):
    return jax.shard_map(
        shards,
        mesh=mesh,
        in_specs=(P("tm", "space"), P()),
        out_specs=(P(), P(None, None, "space"), P("tm", "space")),
        check_vma=False,
    )
```

```python
import jax
import jax.numpy as jnp
from jax import lax
from jax.experimental import pallas as pl
from jax.experimental.pallas import tpu as pltpu
from jax.sharding import PartitionSpec as P

damping = 0.01
MODES = 32
TIMES = 32768
ROWS = 512
COLS = 8192
QUARTER = COLS // 4
PART = QUARTER // 4
WIDTH = 512
ORDER = (1, 3, 2)
COARSE = 256
FINE = TIMES // COARSE
EXACT = lax.Precision.HIGHEST
VMEM = pl.BlockSpec(memory_space=pltpu.VMEM)
PARAMS = pltpu.CompilerParams(vmem_limit_bytes=24 * 1024 * 1024)
WIDE_PARAMS = pltpu.CompilerParams(vmem_limit_bytes=52 * 1024 * 1024)
AXES = {"u": "xz", "v": "yx", "w": "zy"}


def place(device):
    return device >> 5, (device >> 3) & 3, (device >> 1) & 3, device & 1


def shifted(axis, step):
    pairs = []
    for device in range(128):
        z, y, x, core = place(device)
        along = AXES[axis][core]
        if along == "z":
            z = (z + step) % 4
        elif along == "y":
            y = (y + step) % 4
        else:
            x = (x + step) % 4
        pairs.append((device, ((z * 4 + y) * 4 + x) * 2 + core))
    return pairs


def send(value, axis, step):
    return lax.ppermute(value, ("tm", "space"), shifted(axis, step))


def swap_cores(value):
    return lax.ppermute(value, ("tm", "space"), [(d, d ^ 1) for d in range(128)])


def dot(left, right):
    return jnp.dot(left, right, precision=EXACT, preferred_element_type=jnp.float32)


def dot_t(left, right):
    return lax.dot_general(
        left, right, (((1,), (1,)), ((), ())), precision=EXACT, preferred_element_type=jnp.float32
    )


def waves(exponents, times):
    magnitude = jnp.exp(times[None, :] * exponents[0][:, None])
    phase_angle = times[None, :] * exponents[1][:, None]
    return magnitude * jnp.cos(phase_angle), magnitude * jnp.sin(phase_angle)


def basis_kernel(first_ref, exponents_ref, flat_ref, tall_ref):
    row = lax.broadcasted_iota(jnp.int32, (MODES, MODES), 0)
    col = lax.broadcasted_iota(jnp.int32, (MODES, MODES), 1)
    values = exponents_ref[...]
    rate = jnp.sum(jnp.where(row == col, values[0:1], 0.0), 1, keepdims=True)
    frequency = jnp.sum(jnp.where(row == col, values[1:2], 0.0), 1, keepdims=True)
    step = first_ref[0] + lax.broadcasted_iota(jnp.int32, (MODES, ROWS), 1)
    times = step.astype(jnp.float32) * (1.0 / TIMES)
    magnitude = jnp.exp(times * rate)
    phase_angle = times * frequency
    real = magnitude * jnp.cos(phase_angle)
    imag = magnitude * jnp.sin(phase_angle)
    plain = jnp.concatenate([real, imag], 0)
    flat_ref[...] = jnp.concatenate([plain, times * real, times * imag], 0).astype(jnp.bfloat16)
    tall_ref[...] = plain.T.astype(jnp.bfloat16)


def make_basis(first_row, exponents):
    return pl.pallas_call(
        basis_kernel,
        in_specs=[pl.BlockSpec(memory_space=pltpu.SMEM), VMEM],
        out_specs=[VMEM] * 2,
        out_shape=[
            jax.ShapeDtypeStruct((4 * MODES, ROWS), jnp.bfloat16),
            jax.ShapeDtypeStruct((ROWS, 2 * MODES), jnp.bfloat16),
        ],
        compiler_params=PARAMS,
        name="basis",
    )(first_row.astype(jnp.int32), exponents)


def table(exponents, times):
    real, imag = waves(exponents, times)
    both = jnp.concatenate([times, times])[None, :]
    plain = jnp.concatenate([real, imag], 1)
    turned = jnp.concatenate([imag, -real], 1)
    return jnp.stack([plain, turned, both * plain, both * turned])


def complex_product(a, b):
    return a[0] * b[0] - a[1] * b[1], a[0] * b[1] + a[1] * b[0]


def eliminate(real, imag, size):
    row_index = lax.broadcasted_iota(jnp.int32, real.shape, 0)
    for k in range(size):
        inverse_pivot = 1.0 / real[k : k + 1, k : k + 1]
        row_real = real[k : k + 1, :] * inverse_pivot
        row_imag = imag[k : k + 1, :] * inverse_pivot
        col_real = real[:, k : k + 1]
        col_imag = imag[:, k : k + 1]
        next_real = real - (col_real * row_real - col_imag * row_imag)
        next_imag = imag - (col_real * row_imag + col_imag * row_real)
        here = row_index == k
        real = jnp.where(here, row_real, next_real)
        imag = jnp.where(here, row_imag, next_imag)
    return real, imag


def grams(t):
    plain, turned, t_plain, t_turned = t[0], t[1], t[2], t[3]
    g = (dot_t(plain, plain), dot_t(plain, turned))
    c = (dot_t(plain, t_plain), dot_t(plain, t_turned))
    ct = (dot_t(t_plain, plain), dot_t(t_turned, plain))
    e = (dot_t(t_plain, t_plain), dot_t(t_plain, t_turned))
    gt = (dot_t(plain, plain), dot_t(turned, plain))
    return g, c, e, gt, ct


def add(a, b):
    return a[0] + b[0], a[1] + b[1]


def gram_kernel(coarse_ref, fine_ref, solve_ref, terms_ref):
    ga, ca, ea, gta, cta = grams(coarse_ref)
    gb, cb, eb, gtb, ctb = grams(fine_ref)
    g = complex_product(ga, gb)
    c = add(complex_product(ca, gb), complex_product(ga, cb))
    ct = add(complex_product(cta, gtb), complex_product(gta, ctb))
    cross = complex_product(ca, cb)
    e = add(complex_product(ea, gb), complex_product(ga, eb))
    e = (e[0] + 2.0 * cross[0], e[1] + 2.0 * cross[1])
    row = lax.broadcasted_iota(jnp.int32, (MODES, MODES), 0)
    col = lax.broadcasted_iota(jnp.int32, (MODES, MODES), 1)
    one = (row == col).astype(jnp.float32)
    real = jnp.concatenate([g[0], one], 1)
    imag = jnp.concatenate([g[1], jnp.zeros_like(one)], 1)
    real, imag = eliminate(real, imag, MODES)
    inv_real, inv_imag = real[:, MODES:], imag[:, MODES:]
    solve_ref[...] = jnp.concatenate(
        [jnp.concatenate([inv_real, inv_imag], 1), jnp.concatenate([inv_imag, -inv_real], 1)], 0
    )
    d_real = dot(inv_real, c[0]) - dot(inv_imag, c[1])
    d_imag = dot(inv_real, c[1]) + dot(inv_imag, c[0])
    terms_ref[0] = e[0] - (dot(ct[0], d_real) + dot(ct[1], d_imag))
    terms_ref[1] = e[1] - (dot(ct[0], d_imag) - dot(ct[1], d_real))
    terms_ref[2] = ct[0]
    terms_ref[3] = ct[1]


def project_kernel(index_ref, basis_ref, snapshots_ref, *out_refs):
    for step in range(len(out_refs) // 2):

        @pl.when(pl.program_id(0) == step)
        def _():
            found = jnp.dot(
                basis_ref[...], snapshots_ref[...], preferred_element_type=jnp.float32
            )
            for j in range(4):
                out_refs[2 * step + j // 2][j % 2] = found[:, j * PART : (j + 1) * PART]


def project(indices, basis_t, snapshots):
    count = indices.shape[0]
    return pl.pallas_call(
        project_kernel,
        grid_spec=pltpu.PrefetchScalarGridSpec(
            num_scalar_prefetch=1,
            grid=(count,),
            in_specs=[
                pl.BlockSpec((4 * MODES, ROWS), lambda j, i: (0, 0)),
                pl.BlockSpec((ROWS, QUARTER), lambda j, i: (0, i[j])),
            ],
            out_specs=[pl.BlockSpec((2, 4 * MODES, PART), lambda j, i: (0, 0, 0))] * (2 * count),
        ),
        out_shape=[jax.ShapeDtypeStruct((2, 4 * MODES, PART), jnp.float32)] * (2 * count),
        compiler_params=WIDE_PARAMS,
        cost_estimate=pl.CostEstimate(
            flops=count * 2 * 128 * ROWS * QUARTER,
            bytes_accessed=count * (3 << 20),
            transcendentals=0,
        ),
        name="project",
    )(indices, basis_t, snapshots)


def relay_kernel(low_ref, high_ref, from_left_ref, from_right_ref, low_out_ref, high_out_ref):
    low_out_ref[...] = low_ref[...] + from_left_ref[...]
    high_out_ref[...] = high_ref[...] + from_right_ref[...]


def relay(low, high, from_left, from_right):
    return pl.pallas_call(
        relay_kernel,
        in_specs=[VMEM] * 4,
        out_specs=[VMEM] * 2,
        out_shape=[jax.ShapeDtypeStruct((2, 4 * MODES, PART), jnp.float32)] * 2,
        compiler_params=PARAMS,
        name="relay",
    )(low, high, from_left, from_right)


def first_sum_kernel(v_ref, *refs):
    out_refs = refs[6:]
    for step in range(4):
        j = (v_ref[0] + step) & 3
        for half in range(2):

            @pl.when((j >> 1) == half)
            def _():
                a, b, c = (ref[j & 1] for ref in refs[3 * half : 3 * half + 3])
                out_refs[step][...] = (a + b) + c


def first_sum(v, low, high):
    return pl.pallas_call(
        first_sum_kernel,
        in_specs=[pl.BlockSpec(memory_space=pltpu.SMEM)] + [VMEM] * 6,
        out_specs=[VMEM] * 4,
        out_shape=[jax.ShapeDtypeStruct((4 * MODES, PART), jnp.float32)] * 4,
        compiler_params=PARAMS,
        name="first_sum",
    )(v, *low, *high)


def sum_kernel(own_ref, r1_ref, r2_ref, r3_ref, out_ref):
    out_ref[...] = (own_ref[...] + r2_ref[...]) + (r1_ref[...] + r3_ref[...])


def plain_sum(own, received):
    return pl.pallas_call(
        sum_kernel,
        in_specs=[VMEM] * 4,
        out_specs=VMEM,
        out_shape=jax.ShapeDtypeStruct(own.shape, jnp.float32),
        compiler_params=PARAMS,
        name="plain_sum",
    )(own, *received)


def amplitude_kernel(solve_ref, own_ref, r1_ref, r2_ref, r3_ref, out_ref):
    total = (own_ref[...] + r2_ref[...]) + (r1_ref[...] + r3_ref[...])
    amp = dot(solve_ref[...], total[: 2 * MODES])
    out_ref[:, :PART] = amp
    amp_real, amp_imag = amp[:MODES], amp[MODES:]
    z_cos, z_sin = total[2 * MODES : 3 * MODES], total[3 * MODES :]
    v_real = jnp.sum(amp_real * z_cos - amp_imag * z_sin, 1, keepdims=True)
    v_imag = jnp.sum(-amp_real * z_sin - amp_imag * z_cos, 1, keepdims=True)
    v = jnp.concatenate([v_real, v_imag], 0)
    s = dot_t(amp, amp)
    out_ref[:, PART:] = jnp.concatenate([s, jnp.broadcast_to(v, (64, 64))], 1)


def amplitudes_of(solve, own, received):
    return pl.pallas_call(
        amplitude_kernel,
        in_specs=[VMEM] * 5,
        out_specs=VMEM,
        out_shape=jax.ShapeDtypeStruct((2 * MODES, PART + 128), jnp.float32),
        compiler_params=PARAMS,
        name="amplitudes",
    )(solve, own, *received)


def join_kernel(v_ref, own_ref, r1_ref, r2_ref, r3_ref, out_ref):
    for step, ref in enumerate((own_ref, r1_ref, r2_ref, r3_ref)):
        j = (v_ref[0] - step) & 3
        out_ref[:, pl.ds(pl.multiple_of(j * PART, PART), PART)] = ref[:, :PART]
    out_ref[:, QUARTER:] = (own_ref[:, PART:] + r2_ref[:, PART:]) + (
        r1_ref[:, PART:] + r3_ref[:, PART:]
    )


def join(v, own, received):
    return pl.pallas_call(
        join_kernel,
        in_specs=[pl.BlockSpec(memory_space=pltpu.SMEM)] + [VMEM] * 4,
        out_specs=VMEM,
        out_shape=jax.ShapeDtypeStruct((2 * MODES, QUARTER + 128), jnp.float32),
        compiler_params=PARAMS,
        name="join",
    )(v, own, *received)


def columns_of(quarter):
    return pl.ds(pl.multiple_of(quarter * QUARTER, QUARTER), QUARTER)


def fit_piece(basis_ref, amp_ref, snapshots_ref, out_ref):
    for first in range(0, QUARTER, WIDTH):
        here = pl.ds(first, WIDTH)
        amp = amp_ref[:, here]
        signed = jnp.concatenate([amp[:MODES], -amp[MODES:]], 0).astype(jnp.bfloat16)
        fitted = jnp.dot(basis_ref[...], signed, preferred_element_type=jnp.float32)
        out_ref[:, here] = (snapshots_ref[:, here].astype(jnp.float32) - fitted).astype(
            jnp.bfloat16
        )


def own_kernel(
    u_ref, basis_ref, amp_ref, snapshots_ref, residual_ref, amp_out_ref, rest_ref, old, new, sems
):
    own = columns_of(u_ref[0])
    load = pltpu.make_async_copy(snapshots_ref.at[:, own], old, sems.at[0])
    load.start()
    copies = [
        pltpu.make_async_copy(amp_ref.at[:, pl.ds(0, QUARTER)], amp_out_ref.at[:, own], sems.at[1])
    ]
    for n, step in enumerate(ORDER):
        there = columns_of((u_ref[0] - step) & 3)
        copies.append(
            pltpu.make_async_copy(snapshots_ref.at[:, there], rest_ref.at[n], sems.at[2 + n])
        )
    for copy in copies:
        copy.start()
    load.wait()
    fit_piece(basis_ref, amp_ref, old, new)
    store = pltpu.make_async_copy(new, residual_ref.at[:, own], sems.at[0])
    store.start()
    for copy in copies:
        copy.wait()
    store.wait()


def rest_kernel(u_ref, basis_ref, a1, a2, a3, rest_ref, k1, k2, residual_ref, amp_out_ref, new, sems):
    copies = []
    for n, (step, amp_ref) in enumerate(zip(ORDER, (a1, a2, a3))):
        there = columns_of((u_ref[0] - step) & 3)
        copies.append(
            pltpu.make_async_copy(
                amp_ref.at[:, pl.ds(0, QUARTER)], amp_out_ref.at[:, there], sems.at[n]
            )
        )
        copies[-1].start()
    for n, (step, amp_ref) in enumerate(zip(ORDER, (a1, a2, a3))):
        there = columns_of((u_ref[0] - step) & 3)
        fit_piece(basis_ref, amp_ref, rest_ref.at[n], new.at[n])
        copies.append(
            pltpu.make_async_copy(new.at[n], residual_ref.at[:, there], sems.at[3 + n])
        )
        copies[-1].start()
    for copy in copies:
        copy.wait()


SMEM = pl.BlockSpec(memory_space=pltpu.SMEM)
HBM = pl.BlockSpec(memory_space=pltpu.HBM)
RESULTS = [
    jax.ShapeDtypeStruct((ROWS, COLS), jnp.bfloat16),
    jax.ShapeDtypeStruct((2 * MODES, COLS), jnp.float32),
]


def own_residual(u, basis, amp, snapshots):
    return pl.pallas_call(
        own_kernel,
        in_specs=[SMEM, VMEM, VMEM, HBM],
        out_specs=[HBM, HBM, VMEM],
        out_shape=RESULTS + [jax.ShapeDtypeStruct((3, ROWS, QUARTER), jnp.bfloat16)],
        scratch_shapes=[
            pltpu.VMEM((ROWS, QUARTER), jnp.bfloat16),
            pltpu.VMEM((ROWS, QUARTER), jnp.bfloat16),
            pltpu.SemaphoreType.DMA((5,)),
        ],
        compiler_params=PARAMS,
        cost_estimate=pl.CostEstimate(
            flops=2 * 64 * ROWS * QUARTER, bytes_accessed=11 << 20, transcendentals=0
        ),
        name="own_residual",
    )(u, basis, amp, snapshots)


def rest_residual(u, basis, amps, rest, residual, amp_out):
    return pl.pallas_call(
        rest_kernel,
        in_specs=[SMEM, VMEM, VMEM, VMEM, VMEM, VMEM, HBM, HBM],
        out_specs=[HBM, HBM],
        out_shape=RESULTS,
        input_output_aliases={6: 0, 7: 1},
        scratch_shapes=[
            pltpu.VMEM((3, ROWS, QUARTER), jnp.bfloat16),
            pltpu.SemaphoreType.DMA((6,)),
        ],
        compiler_params=PARAMS,
        cost_estimate=pl.CostEstimate(
            flops=6 * 64 * ROWS * QUARTER, bytes_accessed=8 << 20, transcendentals=0
        ),
        name="rest_residual",
    )(u, basis, *amps, rest, residual, amp_out)


def update_kernel(exponents_ref, terms_ref, here_ref, there_ref, out_ref):
    total = here_ref[...] + there_ref[...]
    s_real = total[:MODES, :MODES] + total[MODES:, MODES : 2 * MODES]
    s_imag = total[:MODES, MODES : 2 * MODES] - total[MODES:, :MODES]
    v_real = total[:MODES, 2 * MODES : 2 * MODES + 1]
    v_imag = total[MODES:, 2 * MODES : 2 * MODES + 1]
    m_real, m_imag, ct_real, ct_imag = (terms_ref[i] for i in range(4))
    row = lax.broadcasted_iota(jnp.int32, (MODES, MODES), 0)
    col = lax.broadcasted_iota(jnp.int32, (MODES, MODES), 1)
    one = (row == col).astype(jnp.float32)
    w_real = jnp.sum(ct_real * s_real + ct_imag * s_imag, 1, keepdims=True)
    w_imag = jnp.sum(ct_real * s_imag - ct_imag * s_real, 1, keepdims=True)
    h_real = s_real * m_real - s_imag * m_imag + damping * one
    h_imag = s_real * m_imag + s_imag * m_real
    wide = (MODES, MODES)
    real = jnp.concatenate([h_real, jnp.broadcast_to(w_real - v_real, wide)], 1)
    imag = jnp.concatenate([h_imag, jnp.broadcast_to(w_imag - v_imag, wide)], 1)
    real, imag = eliminate(real, imag, MODES)
    step_real = jnp.sum(one * real[:, MODES:], 0, keepdims=True)
    step_imag = jnp.sum(one * imag[:, MODES:], 0, keepdims=True)
    out_ref[...] = exponents_ref[...] - jnp.concatenate([step_real, step_imag], 0)


def shards(snapshots, exponents):
    z, y, x, core = place(lax.axis_index("tm") * 2 + lax.axis_index("space"))
    u = jnp.where(core == 0, x, z).astype(jnp.int32)
    v = jnp.where(core == 0, y, x).astype(jnp.int32)
    at_v = v[None]
    basis_t, basis = make_basis(lax.axis_index("tm")[None] * ROWS, exponents)

    low, high = project(((u + 2) & 3)[None], basis_t, snapshots)
    from_left = send(low, "u", 1)
    from_right = send(high, "u", 3)
    right_low, right_high, left_low, left_high = project(
        jnp.stack([(u + 1) & 3, (u + 3) & 3]), basis_t, snapshots
    )
    direct_high = send(right_high, "u", 1)
    direct_low = send(left_low, "u", 3)
    right_low, left_high = relay(right_low, left_high, from_left, from_right)
    relayed_low = send(right_low, "u", 1)
    relayed_high = send(left_high, "u", 3)
    own_index, exponents, _ = lax.optimization_barrier((u[None], exponents, right_low))
    own_low, own_high = project(own_index, basis_t, snapshots)

    coarse = table(exponents, jnp.arange(COARSE, dtype=jnp.float32) / COARSE)
    fine = table(exponents, jnp.arange(FINE, dtype=jnp.float32) / TIMES)
    solve, terms = pl.pallas_call(
        gram_kernel,
        in_specs=[VMEM] * 2,
        out_specs=[VMEM] * 2,
        out_shape=[
            jax.ShapeDtypeStruct((2 * MODES, 2 * MODES), jnp.float32),
            jax.ShapeDtypeStruct((4, MODES, MODES), jnp.float32),
        ],
        compiler_params=PARAMS,
        cost_estimate=pl.CostEstimate(
            flops=1 << 30, bytes_accessed=16 << 20, transcendentals=0
        ),
        name="gram",
    )(coarse, fine)

    own_low, solve, terms = lax.optimization_barrier((own_low, solve, terms))
    sums = first_sum(
        at_v, (own_low, relayed_low, direct_low), (own_high, direct_high, relayed_high)
    )
    received = {s: send(sums[s], "v", s) for s in (2, 1, 3)}
    total = plain_sum(sums[0], [received[s] for s in (1, 2, 3)])
    received = {s: send(total, "w", s) for s in (2, 1, 3)}
    amp = amplitudes_of(solve, total, [received[s] for s in (1, 2, 3)])
    received = {s: send(amp, "v", s) for s in (2, 1, 3)}
    amp = join(at_v, amp, [received[s] for s in (1, 2, 3)])
    received = {s: send(amp, "u", s) for s in (2, 1, 3)}
    residual, amp_out, rest = own_residual(u[None], basis, amp, snapshots)
    sums = plain_sum(
        amp[:, QUARTER:], [received[s][:, QUARTER:] for s in (1, 2, 3)]
    )
    other = swap_cores(sums)
    residual, amp_out = rest_residual(
        u[None], basis, [received[step] for step in ORDER], rest, residual, amp_out
    )
    new_exponents = pl.pallas_call(
        update_kernel,
        in_specs=[VMEM] * 4,
        out_specs=VMEM,
        out_shape=jax.ShapeDtypeStruct((2, MODES), jnp.float32),
        compiler_params=PARAMS,
        name="update",
    )(exponents, terms, sums, other)
    return (new_exponents, amp_out.reshape(2, MODES, COLS), residual)


def solution(mesh):
    return jax.shard_map(
        shards,
        mesh=mesh,
        in_specs=(P("tm", "space"), P()),
        out_specs=(P(), P(None, None, "space"), P("tm", "space")),
        check_vma=False,
    )
```

```python
import functools

import jax
import jax.numpy as jnp
from jax import lax
from jax.experimental import pallas as pl
from jax.experimental.pallas import tpu as pltpu
from jax.sharding import PartitionSpec as P

damping = 0.01
MODES = 32
TIMES = 32768
ROWS = 512
COLS = 8192
QUARTER = COLS // 4
PART = QUARTER // 4
WIDTH = 512
ORDER = (1, 3, 2)
COARSE = 256
FINE = TIMES // COARSE
EXACT = lax.Precision.HIGHEST
VMEM = pl.BlockSpec(memory_space=pltpu.VMEM)
PARAMS = pltpu.CompilerParams(vmem_limit_bytes=24 * 1024 * 1024)
WIDE_PARAMS = pltpu.CompilerParams(vmem_limit_bytes=46 * 1024 * 1024)
AXES = {"u": "xz", "v": "yx", "w": "zy"}


def place(device):
    return device >> 5, (device >> 3) & 3, (device >> 1) & 3, device & 1


def shifted(axis, step):
    pairs = []
    for device in range(128):
        z, y, x, core = place(device)
        along = AXES[axis][core]
        if along == "z":
            z = (z + step) % 4
        elif along == "y":
            y = (y + step) % 4
        else:
            x = (x + step) % 4
        pairs.append((device, ((z * 4 + y) * 4 + x) * 2 + core))
    return pairs


def send(value, axis, step):
    return lax.ppermute(value, ("tm", "space"), shifted(axis, step))


def swap_cores(value):
    return lax.ppermute(value, ("tm", "space"), [(d, d ^ 1) for d in range(128)])


def dot(left, right):
    return jnp.dot(left, right, precision=EXACT, preferred_element_type=jnp.float32)


def dot_t(left, right):
    return lax.dot_general(
        left, right, (((1,), (1,)), ((), ())), precision=EXACT, preferred_element_type=jnp.float32
    )


def waves(exponents, times):
    magnitude = jnp.exp(times[None, :] * exponents[0][:, None])
    phase_angle = times[None, :] * exponents[1][:, None]
    return magnitude * jnp.cos(phase_angle), magnitude * jnp.sin(phase_angle)


def basis_kernel(first_ref, exponents_ref, flat_ref, tall_ref):
    row = lax.broadcasted_iota(jnp.int32, (MODES, MODES), 0)
    col = lax.broadcasted_iota(jnp.int32, (MODES, MODES), 1)
    values = exponents_ref[...]
    rate = jnp.sum(jnp.where(row == col, values[0:1], 0.0), 1, keepdims=True)
    frequency = jnp.sum(jnp.where(row == col, values[1:2], 0.0), 1, keepdims=True)
    step = first_ref[0] + lax.broadcasted_iota(jnp.int32, (MODES, ROWS), 1)
    times = step.astype(jnp.float32) * (1.0 / TIMES)
    magnitude = jnp.exp(times * rate)
    phase_angle = times * frequency
    real = magnitude * jnp.cos(phase_angle)
    imag = magnitude * jnp.sin(phase_angle)
    plain = jnp.concatenate([real, imag], 0)
    flat_ref[...] = jnp.concatenate([plain, times * real, times * imag], 0).astype(jnp.bfloat16)
    tall_ref[...] = plain.T.astype(jnp.bfloat16)


def make_basis(first_row, exponents):
    return pl.pallas_call(
        basis_kernel,
        in_specs=[pl.BlockSpec(memory_space=pltpu.SMEM), VMEM],
        out_specs=[VMEM] * 2,
        out_shape=[
            jax.ShapeDtypeStruct((4 * MODES, ROWS), jnp.bfloat16),
            jax.ShapeDtypeStruct((ROWS, 2 * MODES), jnp.bfloat16),
        ],
        compiler_params=PARAMS,
        name="basis",
    )(first_row.astype(jnp.int32), exponents)


def table(exponents, times):
    real, imag = waves(exponents, times)
    both = jnp.concatenate([times, times])[None, :]
    plain = jnp.concatenate([real, imag], 1)
    turned = jnp.concatenate([imag, -real], 1)
    return jnp.stack([plain, turned, both * plain, both * turned])


def complex_product(a, b):
    return a[0] * b[0] - a[1] * b[1], a[0] * b[1] + a[1] * b[0]


def eliminate(real, imag, size):
    row_index = lax.broadcasted_iota(jnp.int32, real.shape, 0)
    wide = (1, real.shape[1])
    for k in range(0, size, 2):
        upper, lower = slice(k, k + 1), slice(k + 1, k + 2)
        inverse_a = 1.0 / jnp.broadcast_to(real[upper, upper], wide)
        b = jnp.broadcast_to(real[lower, lower], wide)
        c_real = jnp.broadcast_to(real[upper, lower], wide)
        c_imag = jnp.broadcast_to(imag[upper, lower], wide)
        l_real = jnp.broadcast_to(real[lower, upper], wide) * inverse_a
        l_imag = jnp.broadcast_to(imag[lower, upper], wide) * inverse_a
        inverse_s = 1.0 / (b - (l_real * c_real - l_imag * c_imag))
        r1, i1, r2, i2 = real[upper], imag[upper], real[lower], imag[lower]
        r2, i2 = (
            (r2 - (l_real * r1 - l_imag * i1)) * inverse_s,
            (i2 - (l_real * i1 + l_imag * r1)) * inverse_s,
        )
        r1, i1 = (
            (r1 - (c_real * r2 - c_imag * i2)) * inverse_a,
            (i1 - (c_real * i2 + c_imag * r2)) * inverse_a,
        )
        p_real, p_imag = real[:, upper], imag[:, upper]
        q_real, q_imag = real[:, lower], imag[:, lower]
        next_real = real - ((p_real * r1 - p_imag * i1) + (q_real * r2 - q_imag * i2))
        next_imag = imag - ((p_real * i1 + p_imag * r1) + (q_real * i2 + q_imag * r2))
        real = jnp.where(row_index == k, r1, jnp.where(row_index == k + 1, r2, next_real))
        imag = jnp.where(row_index == k, i1, jnp.where(row_index == k + 1, i2, next_imag))
    return real, imag


def grams(t):
    plain, turned, t_plain, t_turned = t[0], t[1], t[2], t[3]
    g = (dot_t(plain, plain), dot_t(plain, turned))
    c = (dot_t(plain, t_plain), dot_t(plain, t_turned))
    ct = (dot_t(t_plain, plain), dot_t(t_turned, plain))
    e = (dot_t(t_plain, t_plain), dot_t(t_plain, t_turned))
    gt = (dot_t(plain, plain), dot_t(turned, plain))
    return g, c, e, gt, ct


def add(a, b):
    return a[0] + b[0], a[1] + b[1]


def gram_kernel(coarse_ref, fine_ref, solve_ref, terms_ref):
    ga, ca, ea, gta, cta = grams(coarse_ref)
    gb, cb, eb, gtb, ctb = grams(fine_ref)
    g = complex_product(ga, gb)
    c = add(complex_product(ca, gb), complex_product(ga, cb))
    ct = add(complex_product(cta, gtb), complex_product(gta, ctb))
    cross = complex_product(ca, cb)
    e = add(complex_product(ea, gb), complex_product(ga, eb))
    e = (e[0] + 2.0 * cross[0], e[1] + 2.0 * cross[1])
    row = lax.broadcasted_iota(jnp.int32, (MODES, MODES), 0)
    col = lax.broadcasted_iota(jnp.int32, (MODES, MODES), 1)
    one = (row == col).astype(jnp.float32)
    real = jnp.concatenate([g[0], one], 1)
    imag = jnp.concatenate([g[1], jnp.zeros_like(one)], 1)
    real, imag = eliminate(real, imag, MODES)
    inv_real, inv_imag = real[:, MODES:], imag[:, MODES:]
    solve_ref[...] = jnp.concatenate(
        [jnp.concatenate([inv_real, inv_imag], 1), jnp.concatenate([inv_imag, -inv_real], 1)], 0
    )
    d_real = dot(inv_real, c[0]) - dot(inv_imag, c[1])
    d_imag = dot(inv_real, c[1]) + dot(inv_imag, c[0])
    terms_ref[0] = e[0] - (dot(ct[0], d_real) + dot(ct[1], d_imag))
    terms_ref[1] = e[1] - (dot(ct[0], d_imag) - dot(ct[1], d_real))
    terms_ref[2] = ct[0]
    terms_ref[3] = ct[1]


def project_kernel(index_ref, basis_ref, snapshots_ref, *out_refs):
    for step in range(len(out_refs) // 2):

        @pl.when(pl.program_id(0) == step)
        def _():
            found = jnp.dot(
                basis_ref[...], snapshots_ref[...], preferred_element_type=jnp.float32
            )
            for j in range(4):
                out_refs[2 * step + j // 2][j % 2] = found[:, j * PART : (j + 1) * PART]


def project(indices, basis_t, snapshots):
    count = indices.shape[0]
    return pl.pallas_call(
        project_kernel,
        grid_spec=pltpu.PrefetchScalarGridSpec(
            num_scalar_prefetch=1,
            grid=(count,),
            in_specs=[
                pl.BlockSpec((4 * MODES, ROWS), lambda j, i: (0, 0)),
                pl.BlockSpec((ROWS, QUARTER), lambda j, i: (0, i[j])),
            ],
            out_specs=[pl.BlockSpec((2, 4 * MODES, PART), lambda j, i: (0, 0, 0))] * (2 * count),
        ),
        out_shape=[jax.ShapeDtypeStruct((2, 4 * MODES, PART), jnp.float32)] * (2 * count),
        compiler_params=WIDE_PARAMS,
        cost_estimate=pl.CostEstimate(
            flops=count * 2 * 128 * ROWS * QUARTER,
            bytes_accessed=count * (3 << 20),
            transcendentals=0,
        ),
        name="project",
    )(indices, basis_t, snapshots)


def relay_kernel(low_ref, high_ref, from_left_ref, from_right_ref, low_out_ref, high_out_ref):
    low_out_ref[...] = low_ref[...] + from_left_ref[...]
    high_out_ref[...] = high_ref[...] + from_right_ref[...]


def relay(low, high, from_left, from_right):
    return pl.pallas_call(
        relay_kernel,
        in_specs=[VMEM] * 4,
        out_specs=[VMEM] * 2,
        out_shape=[jax.ShapeDtypeStruct((2, 4 * MODES, PART), jnp.float32)] * 2,
        compiler_params=PARAMS,
        name="relay",
    )(low, high, from_left, from_right)


def first_sum_kernel(v_ref, *refs):
    out_refs = refs[6:]
    for step in range(4):
        j = (v_ref[0] + step) & 3
        for half in range(2):

            @pl.when((j >> 1) == half)
            def _():
                a, b, c = (ref[j & 1] for ref in refs[3 * half : 3 * half + 3])
                out_refs[step][...] = (a + b) + c


def first_sum(v, low, high):
    return pl.pallas_call(
        first_sum_kernel,
        in_specs=[pl.BlockSpec(memory_space=pltpu.SMEM)] + [VMEM] * 6,
        out_specs=[VMEM] * 4,
        out_shape=[jax.ShapeDtypeStruct((4 * MODES, PART), jnp.float32)] * 4,
        compiler_params=PARAMS,
        name="first_sum",
    )(v, *low, *high)


def sum_kernel(own_ref, r1_ref, r2_ref, r3_ref, out_ref):
    out_ref[...] = (own_ref[...] + r2_ref[...]) + (r1_ref[...] + r3_ref[...])


def plain_sum(own, received):
    return pl.pallas_call(
        sum_kernel,
        in_specs=[VMEM] * 4,
        out_specs=VMEM,
        out_shape=jax.ShapeDtypeStruct(own.shape, jnp.float32),
        compiler_params=PARAMS,
        name="plain_sum",
    )(own, *received)


def amplitude_kernel(solve_ref, own_ref, r1_ref, r2_ref, r3_ref, out_ref):
    total = (own_ref[...] + r2_ref[...]) + (r1_ref[...] + r3_ref[...])
    amp = dot(solve_ref[...], total[: 2 * MODES])
    out_ref[:, :PART] = amp
    amp_real, amp_imag = amp[:MODES], amp[MODES:]
    z_cos, z_sin = total[2 * MODES : 3 * MODES], total[3 * MODES :]
    v_real = jnp.sum(amp_real * z_cos - amp_imag * z_sin, 1, keepdims=True)
    v_imag = jnp.sum(-amp_real * z_sin - amp_imag * z_cos, 1, keepdims=True)
    v = jnp.concatenate([v_real, v_imag], 0)
    s = dot_t(amp, amp)
    out_ref[:, PART:] = jnp.concatenate([s, jnp.broadcast_to(v, (64, 64))], 1)


def amplitudes_of(solve, own, received):
    return pl.pallas_call(
        amplitude_kernel,
        in_specs=[VMEM] * 5,
        out_specs=VMEM,
        out_shape=jax.ShapeDtypeStruct((2 * MODES, PART + 128), jnp.float32),
        compiler_params=PARAMS,
        name="amplitudes",
    )(solve, own, *received)


def join_kernel(v_ref, own_ref, r1_ref, r2_ref, r3_ref, out_ref):
    for step, ref in enumerate((own_ref, r1_ref, r2_ref, r3_ref)):
        j = (v_ref[0] - step) & 3
        out_ref[:, pl.ds(pl.multiple_of(j * PART, PART), PART)] = ref[:, :PART]
    out_ref[:, QUARTER:] = (own_ref[:, PART:] + r2_ref[:, PART:]) + (
        r1_ref[:, PART:] + r3_ref[:, PART:]
    )


def join(v, own, received):
    return pl.pallas_call(
        join_kernel,
        in_specs=[pl.BlockSpec(memory_space=pltpu.SMEM)] + [VMEM] * 4,
        out_specs=VMEM,
        out_shape=jax.ShapeDtypeStruct((2 * MODES, QUARTER + 128), jnp.float32),
        compiler_params=PARAMS,
        name="join",
    )(v, own, *received)


def columns_of(quarter):
    return pl.ds(pl.multiple_of(quarter * QUARTER, QUARTER), QUARTER)


def fit_piece(basis_ref, amp_ref, snapshots_ref, out_ref):
    for first in range(0, QUARTER, WIDTH):
        here = pl.ds(first, WIDTH)
        amp = amp_ref[:, here]
        signed = jnp.concatenate([amp[:MODES], -amp[MODES:]], 0).astype(jnp.bfloat16)
        fitted = jnp.dot(basis_ref[...], signed, preferred_element_type=jnp.float32)
        out_ref[:, here] = (snapshots_ref[:, here].astype(jnp.float32) - fitted).astype(
            jnp.bfloat16
        )


def own_kernel(
    u_ref, basis_ref, amp_ref, snapshots_ref, residual_ref, amp_out_ref, rest_ref, old, new, sems
):
    own = columns_of(u_ref[0])
    load = pltpu.make_async_copy(snapshots_ref.at[:, own], old, sems.at[0])
    load.start()
    copies = [
        pltpu.make_async_copy(amp_ref.at[:, pl.ds(0, QUARTER)], amp_out_ref.at[:, own], sems.at[1])
    ]
    for n, step in enumerate(ORDER):
        there = columns_of((u_ref[0] - step) & 3)
        copies.append(
            pltpu.make_async_copy(snapshots_ref.at[:, there], rest_ref.at[n], sems.at[2 + n])
        )
    for copy in copies:
        copy.start()
    load.wait()
    fit_piece(basis_ref, amp_ref, old, new)
    store = pltpu.make_async_copy(new, residual_ref.at[:, own], sems.at[0])
    store.start()
    for copy in copies:
        copy.wait()
    store.wait()


def rest_kernel(places, u_ref, basis_ref, rest_ref, *refs):
    count = len(places)
    amp_refs = refs[:count]
    residual_ref, amp_out_ref, new, sems = refs[-4:]
    copies = []
    for n, at in enumerate(places):
        there = columns_of((u_ref[0] - ORDER[at]) & 3)
        copies.append(
            pltpu.make_async_copy(
                amp_refs[n].at[:, pl.ds(0, QUARTER)], amp_out_ref.at[:, there], sems.at[n]
            )
        )
        copies[-1].start()
    for n, at in enumerate(places):
        there = columns_of((u_ref[0] - ORDER[at]) & 3)
        fit_piece(basis_ref, amp_refs[n], rest_ref.at[at], new.at[n])
        copies.append(
            pltpu.make_async_copy(new.at[n], residual_ref.at[:, there], sems.at[count + n])
        )
        copies[-1].start()
    for copy in copies:
        copy.wait()


SMEM = pl.BlockSpec(memory_space=pltpu.SMEM)
HBM = pl.BlockSpec(memory_space=pltpu.HBM)
RESULTS = [
    jax.ShapeDtypeStruct((ROWS, COLS), jnp.bfloat16),
    jax.ShapeDtypeStruct((2 * MODES, COLS), jnp.float32),
]


def own_residual(u, basis, amp, snapshots):
    return pl.pallas_call(
        own_kernel,
        in_specs=[SMEM, VMEM, VMEM, HBM],
        out_specs=[HBM, HBM, VMEM],
        out_shape=RESULTS + [jax.ShapeDtypeStruct((3, ROWS, QUARTER), jnp.bfloat16)],
        scratch_shapes=[
            pltpu.VMEM((ROWS, QUARTER), jnp.bfloat16),
            pltpu.VMEM((ROWS, QUARTER), jnp.bfloat16),
            pltpu.SemaphoreType.DMA((5,)),
        ],
        compiler_params=PARAMS,
        cost_estimate=pl.CostEstimate(
            flops=2 * 64 * ROWS * QUARTER, bytes_accessed=11 << 20, transcendentals=0
        ),
        name="own_residual",
    )(u, basis, amp, snapshots)


def rest_residual(places, u, basis, rest, amps, residual, amp_out):
    count = len(places)
    return pl.pallas_call(
        functools.partial(rest_kernel, places),
        in_specs=[SMEM] + [VMEM] * (2 + count) + [HBM, HBM],
        out_specs=[HBM, HBM],
        out_shape=RESULTS,
        input_output_aliases={3 + count: 0, 4 + count: 1},
        scratch_shapes=[
            pltpu.VMEM((count, ROWS, QUARTER), jnp.bfloat16),
            pltpu.SemaphoreType.DMA((2 * count,)),
        ],
        compiler_params=PARAMS,
        cost_estimate=pl.CostEstimate(
            flops=2 * count * 64 * ROWS * QUARTER, bytes_accessed=count * (5 << 19), transcendentals=0
        ),
        name="rest_residual",
    )(u, basis, rest, *amps, residual, amp_out)


def update_kernel(exponents_ref, terms_ref, here_ref, there_ref, out_ref):
    total = here_ref[...] + there_ref[...]
    s_real = total[:MODES, :MODES] + total[MODES:, MODES : 2 * MODES]
    s_imag = total[:MODES, MODES : 2 * MODES] - total[MODES:, :MODES]
    v_real = total[:MODES, 2 * MODES : 2 * MODES + 1]
    v_imag = total[MODES:, 2 * MODES : 2 * MODES + 1]
    m_real, m_imag, ct_real, ct_imag = (terms_ref[i] for i in range(4))
    row = lax.broadcasted_iota(jnp.int32, (MODES, MODES), 0)
    col = lax.broadcasted_iota(jnp.int32, (MODES, MODES), 1)
    one = (row == col).astype(jnp.float32)
    w_real = jnp.sum(ct_real * s_real + ct_imag * s_imag, 1, keepdims=True)
    w_imag = jnp.sum(ct_real * s_imag - ct_imag * s_real, 1, keepdims=True)
    h_real = s_real * m_real - s_imag * m_imag + damping * one
    h_imag = s_real * m_imag + s_imag * m_real
    wide = (MODES, MODES)
    real = jnp.concatenate([h_real, jnp.broadcast_to(w_real - v_real, wide)], 1)
    imag = jnp.concatenate([h_imag, jnp.broadcast_to(w_imag - v_imag, wide)], 1)
    real, imag = eliminate(real, imag, MODES)
    step_real = jnp.sum(one * real[:, MODES:], 0, keepdims=True)
    step_imag = jnp.sum(one * imag[:, MODES:], 0, keepdims=True)
    out_ref[...] = exponents_ref[...] - jnp.concatenate([step_real, step_imag], 0)


def shards(snapshots, exponents):
    z, y, x, core = place(lax.axis_index("tm") * 2 + lax.axis_index("space"))
    u = jnp.where(core == 0, x, z).astype(jnp.int32)
    v = jnp.where(core == 0, y, x).astype(jnp.int32)
    at_v = v[None]
    basis_t, basis = make_basis(lax.axis_index("tm")[None] * ROWS, exponents)

    low, high = project(((u + 2) & 3)[None], basis_t, snapshots)
    from_left = send(low, "u", 1)
    from_right = send(high, "u", 3)
    right_low, right_high, left_low, left_high = project(
        jnp.stack([(u + 1) & 3, (u + 3) & 3]), basis_t, snapshots
    )
    direct_high = send(right_high, "u", 1)
    direct_low = send(left_low, "u", 3)
    right_low, left_high = relay(right_low, left_high, from_left, from_right)
    relayed_low = send(right_low, "u", 1)
    relayed_high = send(left_high, "u", 3)
    own_index, exponents, _ = lax.optimization_barrier((u[None], exponents, right_low))
    own_low, own_high = project(own_index, basis_t, snapshots)

    coarse = table(exponents, jnp.arange(COARSE, dtype=jnp.float32) / COARSE)
    fine = table(exponents, jnp.arange(FINE, dtype=jnp.float32) / TIMES)
    solve, terms = pl.pallas_call(
        gram_kernel,
        in_specs=[VMEM] * 2,
        out_specs=[VMEM] * 2,
        out_shape=[
            jax.ShapeDtypeStruct((2 * MODES, 2 * MODES), jnp.float32),
            jax.ShapeDtypeStruct((4, MODES, MODES), jnp.float32),
        ],
        compiler_params=PARAMS,
        cost_estimate=pl.CostEstimate(
            flops=1 << 30, bytes_accessed=16 << 20, transcendentals=0
        ),
        name="gram",
    )(coarse, fine)

    own_low, solve, terms = lax.optimization_barrier((own_low, solve, terms))
    sums = first_sum(
        at_v, (own_low, relayed_low, direct_low), (own_high, direct_high, relayed_high)
    )
    received = {s: send(sums[s], "v", s) for s in (2, 1, 3)}
    total = plain_sum(sums[0], [received[s] for s in (1, 2, 3)])
    received = {s: send(total, "w", s) for s in (2, 1, 3)}
    amp = amplitudes_of(solve, total, [received[s] for s in (1, 2, 3)])
    received = {s: send(amp, "v", s) for s in (2, 1, 3)}
    amp = join(at_v, amp, [received[s] for s in (1, 2, 3)])
    received = {s: send(amp, "u", s) for s in (2, 1, 3)}
    residual, amp_out, rest = own_residual(u[None], basis, amp, snapshots)
    residual, amp_out = rest_residual(
        (1, 2), u[None], basis, rest, [received[3], received[2]], residual, amp_out
    )
    ends = [received[s][:, QUARTER:] for s in (1, 2, 3)]
    ends[2], residual = lax.optimization_barrier((ends[2], residual))
    sums = plain_sum(amp[:, QUARTER:], ends)
    other = swap_cores(sums)
    residual, amp_out = rest_residual(
        (0,), u[None], basis, rest, [received[1]], residual, amp_out
    )
    new_exponents = pl.pallas_call(
        update_kernel,
        in_specs=[VMEM] * 4,
        out_specs=VMEM,
        out_shape=jax.ShapeDtypeStruct((2, MODES), jnp.float32),
        compiler_params=PARAMS,
        name="update",
    )(exponents, terms, sums, other)
    return (new_exponents, amp_out.reshape(2, MODES, COLS), residual)


def solution(mesh):
    return jax.shard_map(
        shards,
        mesh=mesh,
        in_specs=(P("tm", "space"), P()),
        out_specs=(P(), P(None, None, "space"), P("tm", "space")),
        check_vma=False,
    )
```
